512 devices in a mesh: tm: 16 (over y, x_hi, core), tile: 32 (over x_lo, z).
Axes of the slice: x: 4 (x_hi: 2, x_lo: 2; x = x_hi * 2 + x_lo), y: 4, z: 16, core: 2. Of those that a mesh axis runs over, the one named last changes fastest.
Arguments:
- latent: bfloat16 [16, 512, 256], P('tm', 'tile'), may hold values from -48 to 48
- conv_weight: bfloat16 [512, 4, 4, 4, 512], P('tile'), may hold values from -0.09375 to 0.09375
- conv_bias: float32 [512], P('tile'), may hold values from -3 to 3
- query_weight: bfloat16 [16, 128, 128], replicated, may hold values from -3 to 3
- key_weight: bfloat16 [16, 128, 128], replicated, may hold values from -3 to 3
Outputs:
- attended: bfloat16 [512, 256, 128], P(('tm', 'tile'))
The draws below stay inside these ranges and needn't reach their ends.
All inputs are finite; a program needn't handle non-finite values.
Results may differ from the reference program's by a relative error of at most 0.0085.
Values may be sent and summed in bfloat16 or wider, within the bound.
No kernel may reach another device: no remote copies, remote signals or barrier semaphores. Data moves between devices by JAX's collectives and lax.ppermute only.
A program may use at most 64 MiB of HBM per device.

```python
import jax
import jax.numpy as jnp
from jax import lax

C = 512
HEADS = 16
HC = 32
HD = 128
SIDE = 16
LFRAMES = 16
OFR = 32
PATCHES = 256
QSPLIT = 1


def draw_latent(key, part):
    key = jax.random.fold_in(key, 1)
    base_key = jax.random.fold_in(key, 0)
    base = jax.random.truncated_normal(base_key, -6.0, 6.0, (LFRAMES, C, SIDE * SIDE), jnp.float32)
    return base.astype(jnp.bfloat16)


def projection_draw(key):
    noise = jax.random.truncated_normal(key, -4.0, 4.0, (HEADS, HD, HD), jnp.float32) * HD ** (-0.5)
    return noise.astype(jnp.bfloat16)


def draw_query_weight(key, part):
    key = jax.random.fold_in(key, 2)
    return projection_draw(key)


def draw_key_weight(key, part):
    key = jax.random.fold_in(key, 3)
    return projection_draw(key)


def steps_of(stream_key, extent, cuts, smallest, high):
    gain, own = 1.0, jax.random.fold_in(stream_key, 6)
    for position, shards_of in cuts:
        draws = jnp.exp(jax.random.uniform(jax.random.fold_in(own, position), (shards_of,), jnp.float32, smallest / len(cuts), high / len(cuts)))
        gain = gain * jnp.repeat(draws, extent[position] // shards_of).reshape([-1 if axis == position else 1 for axis in range(len(extent))])
    return gain


def bell_draw(key, shape, width, limit, shards=(), kind=jnp.bfloat16):
    values = width * jax.random.normal(key, shape, jnp.float32)
    if shards:
        values = values * steps_of(key, shape, shards, -0.22, 0.18)
    return jnp.clip(values, -limit, limit).astype(kind)


def setup_inputs(seed: int = 0) -> dict:
    seeds = jax.random.split(jax.random.key(seed), 6)
    latent = draw_latent(jax.random.fold_in(seeds[5], 71), 0)
    conv_weight = bell_draw(seeds[1], (C, 4, 4, 4, C), (8 * C) ** -0.5, 0.09375, ((0, 32),))
    conv_bias = bell_draw(seeds[2], (C,), 0.5, 3.0, ((0, 32),), jnp.float32)
    query_weight = draw_query_weight(jax.random.fold_in(seeds[5], 71), 0)
    key_weight = draw_key_weight(jax.random.fold_in(seeds[5], 71), 0)
    return {"latent": latent, "conv_weight": conv_weight, "conv_bias": conv_bias, "query_weight": query_weight, "key_weight": key_weight}


def spread_taps(products, side_cells):
    combined = 0.0
    for shift_y in (0, 1):
        for shift_x in (0, 1):
            piece_term = products[:, :, shift_y, :, shift_x, :, :, :]
            piece_term = jnp.transpose(piece_term, (0, 1, 4, 2, 5, 3))
            piece_term = jnp.pad(piece_term, ((0, 0), (0, 0), (shift_y, 1 - shift_y), (0, 0), (shift_x, 1 - shift_x), (0, 0)))
            combined = combined + piece_term
    channels = products.shape[0]
    tap_count = products.shape[1]
    cropped = combined.reshape(channels, tap_count, 2 * side_cells + 2, 2 * side_cells + 2)[:, :, 1:-1, 1:-1]
    return cropped.reshape(channels, tap_count, 4 * side_cells * side_cells)


def conv_taps(latent_plane, weight_rows, side_cells):
    channels = weight_rows.shape[0]
    tap_count = weight_rows.shape[1]
    products = jnp.dot(weight_rows.reshape(-1, weight_rows.shape[-1]).astype(jnp.float32), latent_plane.astype(jnp.float32), precision=lax.Precision.HIGHEST)
    products = products.reshape(channels, tap_count, 2, 2, 2, 2, side_cells, side_cells)
    return spread_taps(products, side_cells)


def attend_pair(token_rows, query_rows, key_rows):
    token_wide = token_rows.astype(jnp.float32)
    queries = jnp.dot(token_wide, query_rows.astype(jnp.float32), precision=lax.Precision.HIGHEST).astype(jnp.bfloat16)
    projected = jnp.dot(token_wide, key_rows.astype(jnp.float32), precision=lax.Precision.HIGHEST).astype(jnp.bfloat16)
    scores = jnp.dot(queries.astype(jnp.float32), projected.astype(jnp.float32).T, precision=lax.Precision.HIGHEST) * (token_rows.shape[1] ** -0.5)
    weights = jax.nn.softmax(scores, axis=-1).astype(jnp.bfloat16)
    mixed = jnp.dot(weights.astype(jnp.float32), token_wide, precision=lax.Precision.HIGHEST)
    return (token_wide + mixed).astype(jnp.bfloat16)


def reference(latent, conv_weight, conv_bias, query_weight, key_weight):
    pixels = 4 * SIDE * SIDE

    def one_frame(latent_plane):
        return conv_taps(latent_plane, conv_weight, SIDE)

    contrib = lax.map(one_frame, latent)
    earlier = jnp.pad(contrib[:-1, :, 3], ((1, 0), (0, 0), (0, 0)))
    later = jnp.pad(contrib[1:, :, 0], ((0, 1), (0, 0), (0, 0)))
    first = contrib[:, :, 1] + earlier
    second = contrib[:, :, 2] + later
    summed = jnp.stack([first, second], 1)
    summed = summed + conv_bias[None, None, :, None]
    frames = summed.astype(jnp.bfloat16).reshape(OFR, C, pixels)
    tokens = frames.reshape(OFR, HC, HEADS, SIDE, 2, SIDE, 2)
    tokens = jnp.transpose(tokens, (0, 2, 3, 5, 4, 6, 1)).reshape(OFR * HEADS, SIDE * SIDE, HD)
    head_ids = jnp.arange(OFR * HEADS, dtype=jnp.int32) % HEADS

    def one_pair(items):
        token_rows, head_id = items
        return attend_pair(token_rows, query_weight[head_id], key_weight[head_id])

    result = lax.map(one_pair, (tokens, head_ids))
    return result.reshape(OFR * HEADS * QSPLIT, PATCHES // QSPLIT, HD)
```

```python
import jax
import jax.numpy as jnp
from jax import lax
from jax.experimental import pallas as pl
from jax.experimental.pallas import tpu as pltpu
from jax.sharding import Mesh, PartitionSpec as P

HEADS = 16
SIDE = 16
CELLS = SIDE * SIDE
TM = ("pair", "core")
VMEM_LIMIT = 32 * 1024 * 1024


def spread(tap_slabs, channels):
    lane = lax.broadcasted_iota(jnp.int32, (channels, CELLS), 1)
    row, col = lane // SIDE, lane % SIDE
    for pa in (0, 1):
        for pb in (0, 1):
            total = None
            for ky, dy in ((1, 0), (3, -1)) if pa == 0 else ((2, 0), (0, 1)):
                for kx, dx in ((1, 0), (3, -1)) if pb == 0 else ((2, 0), (0, 1)):
                    slab = tap_slabs(ky, kx)
                    step = dy * SIDE + dx
                    if step:
                        slab = pltpu.roll(slab, (-step) % CELLS, 1)
                        inside = (row + dy >= 0) & (row + dy < SIDE) & (col + dx >= 0) & (col + dx < SIDE)
                        slab = jnp.where(inside, slab, 0.0)
                    total = slab if total is None else total + slab
            yield pa, pb, total


def conv_kernel(core_ref, weight_ref, latent_ref, bias_ref, own_ref, near_ref, far_ref, later_ref, earlier_ref):
    channels = bias_ref.shape[0]
    rows = 16 * channels
    latent = latent_ref[...]
    for kt in (3, 0, 1, 2):
        products = jnp.dot(
            weight_ref[kt * rows : (kt + 1) * rows, :], latent, preferred_element_type=jnp.float32
        )

        def tap(ky, kx):
            start = (ky * 4 + kx) * channels
            return products[start : start + channels, :]

        for pa, pb, total in spread(tap, channels):
            if kt in (1, 2):
                total = total + bias_ref[...]
            for half in (0, 1):
                piece = total[:, half * 128 : (half + 1) * 128]
                place = (pa * 2 + pb) * 2 + half
                if kt == 3:
                    later_ref[:, place, :] = piece
                elif kt == 0:
                    earlier_ref[:, place, :] = piece
                else:
                    own_ref[kt - 1, :, place, :] = piece
    first = core_ref[0] == 0
    later, earlier = later_ref[...], earlier_ref[...]
    near_ref[...] = jnp.where(first, later, earlier).astype(jnp.bfloat16)
    far_ref[...] = jnp.where(first, earlier, later).astype(jnp.bfloat16)


def attend_kernel(piece_ref, query_ref, key_ref, out_ref, wide_ref, turned_ref):
    wide_ref[...] = piece_ref[...].astype(jnp.float32)
    channels = wide_ref.shape[0]
    for place in range(8):
        parity, half = place // 2, place % 2
        turned_ref[parity * channels : (parity + 1) * channels, half * 128 : (half + 1) * 128] = wide_ref[:, place, :]
    wide = turned_ref[...].T
    tokens = wide.astype(jnp.bfloat16)
    queries = jnp.dot(tokens, query_ref[...], preferred_element_type=jnp.float32).astype(jnp.bfloat16)
    keys = jnp.dot(tokens, key_ref[...], preferred_element_type=jnp.float32).astype(jnp.bfloat16)
    scores = lax.dot_general(queries, keys, (((1,), (1,)), ((), ())), preferred_element_type=jnp.float32)
    scores = scores * (tokens.shape[1] ** -0.5)
    raised = jnp.exp(scores - jnp.max(scores, axis=1, keepdims=True))
    weights = (raised / jnp.sum(raised, axis=1, keepdims=True)).astype(jnp.bfloat16)
    mixed = jnp.dot(weights, tokens, preferred_element_type=jnp.float32)
    out_ref[...] = (wide + mixed).astype(jnp.bfloat16)


def local(latent, conv_weight, conv_bias, query_weight, key_weight):
    tiles = lax.axis_size("tile")
    channels = conv_weight.shape[0]
    core = lax.axis_index("core").astype(jnp.int32)
    copies = jnp.broadcast_to(latent, (tiles,) + latent.shape[1:])
    gathered = lax.all_to_all(copies, "tile", split_axis=0, concat_axis=0, tiled=True)
    gathered = gathered.reshape(-1, CELLS)
    rows = jnp.transpose(conv_weight, (1, 2, 3, 0, 4)).reshape(-1, conv_weight.shape[-1])
    head = lax.axis_index("tile") % HEADS
    query_rows = lax.dynamic_index_in_dim(query_weight, head, 0, keepdims=False)
    key_rows = lax.dynamic_index_in_dim(key_weight, head, 0, keepdims=False)

    edge = jax.ShapeDtypeStruct((channels, 8, 128), jnp.bfloat16)
    own, near, far = pl.pallas_call(
        conv_kernel,
        out_shape=(jax.ShapeDtypeStruct((2, channels, 8, 128), jnp.float32), edge, edge),
        in_specs=[pl.BlockSpec(memory_space=pltpu.SMEM)] + [pl.BlockSpec(memory_space=pltpu.VMEM)] * 3,
        out_specs=[pl.BlockSpec(memory_space=pltpu.VMEM)] * 3,
        scratch_shapes=[pltpu.VMEM((channels, 8, 128), jnp.float32)] * 2,
        compiler_params=pltpu.CompilerParams(vmem_limit_bytes=VMEM_LIMIT),
        name="conv",
    )(core.reshape(1), rows, gathered, conv_bias.reshape(channels, 1))

    groups = lax.axis_size("pair") * lax.axis_size("core")
    route = [(t, t + 1) for t in range(1, groups - 1, 2)] + [(t + 1, t) for t in range(1, groups - 1, 2)]
    from_far = lax.ppermute(far, TM, route)
    both = lax.all_gather(near, "core", axis=0)
    from_near = jnp.where(core == 0, both[1], both[0])
    to_first = jnp.where(core == 0, from_far, from_near).astype(jnp.float32)
    to_second = jnp.where(core == 0, from_near, from_far).astype(jnp.float32)
    frames = (own + jnp.stack([to_first, to_second])).astype(jnp.bfloat16)
    received = lax.all_to_all(
        frames.reshape(2 * channels, 8, 128), "tile", split_axis=0, concat_axis=0, tiled=True
    )
    vmem = pl.BlockSpec(memory_space=pltpu.VMEM)
    attended = pl.pallas_call(
        attend_kernel,
        out_shape=jax.ShapeDtypeStruct((CELLS, 4 * tiles), jnp.bfloat16),
        in_specs=[vmem] * 3,
        out_specs=vmem,
        scratch_shapes=[pltpu.VMEM((tiles, 8, 128), jnp.float32), pltpu.VMEM((4 * tiles, CELLS), jnp.float32)],
        compiler_params=pltpu.CompilerParams(vmem_limit_bytes=VMEM_LIMIT),
        name="attend",
    )(received, query_rows, key_rows)
    return attended[None]


def solution(mesh):
    split = Mesh(mesh.devices.reshape(-1, 2, mesh.devices.shape[1]), ("pair", "core", "tile"))
    in_specs = (P(TM, "tile", None), P("tile", None, None, None, None), P("tile"), P(), P())
    out_specs = P(TM + ("tile",), None, None)
    return jax.shard_map(local, mesh=split, in_specs=in_specs, out_specs=out_specs, check_vma=False)
```

```python
import jax
import jax.numpy as jnp
from jax import lax
from jax.experimental import pallas as pl
from jax.experimental.pallas import tpu as pltpu
from jax.sharding import Mesh, PartitionSpec as P

HEADS = 16
SIDE = 16
CELLS = SIDE * SIDE
TM = ("pair", "core")
VMEM_LIMIT = 32 * 1024 * 1024


def turned(order):
    half = order // 2
    tiles = [start + (z + half // 2) % half for start in (0, half) for z in range(half)]
    return tiles, [tiles.index(tile) for tile in range(order)]


def in_turn(blocks, places):
    return jnp.concatenate([blocks[place] for place in places], 0)


def spread(tap_slabs, channels):
    lane = lax.broadcasted_iota(jnp.int32, (channels, CELLS), 1)
    row, col = lane // SIDE, lane % SIDE
    for pa in (0, 1):
        for pb in (0, 1):
            total = None
            for ky, dy in ((1, 0), (3, -1)) if pa == 0 else ((2, 0), (0, 1)):
                for kx, dx in ((1, 0), (3, -1)) if pb == 0 else ((2, 0), (0, 1)):
                    slab = tap_slabs(ky, kx)
                    step = dy * SIDE + dx
                    if step:
                        slab = pltpu.roll(slab, (-step) % CELLS, 1)
                        inside = (row + dy >= 0) & (row + dy < SIDE) & (col + dx >= 0) & (col + dx < SIDE)
                        slab = jnp.where(inside, slab, 0.0)
                    total = slab if total is None else total + slab
            yield pa, pb, total


def conv_kernel(core_ref, weight_ref, latent_ref, bias_ref, own_ref, near_ref, far_ref, later_ref, earlier_ref):
    channels = bias_ref.shape[0]
    rows = 16 * channels
    _, places = turned(latent_ref.shape[0])
    latent = in_turn(latent_ref, places)
    for kt in (3, 0, 1, 2):
        products = jnp.dot(
            weight_ref[kt * rows : (kt + 1) * rows, :], latent, preferred_element_type=jnp.float32
        )

        def tap(ky, kx):
            start = (ky * 4 + kx) * channels
            return products[start : start + channels, :]

        for pa, pb, total in spread(tap, channels):
            if kt in (1, 2):
                total = total + bias_ref[...]
            for half in (0, 1):
                piece = total[:, half * 128 : (half + 1) * 128]
                place = (pa * 2 + pb) * 2 + half
                if kt == 3:
                    later_ref[:, place, :] = piece
                elif kt == 0:
                    earlier_ref[:, place, :] = piece
                else:
                    middle = channels // 2
                    own_ref[kt - 1, :middle, place, :] = piece[middle:]
                    own_ref[kt - 1, middle:, place, :] = piece[:middle]
    first = core_ref[0] == 0
    middle = channels // 2
    later = jnp.concatenate([later_ref[middle:], later_ref[:middle]], 0)
    earlier = jnp.concatenate([earlier_ref[middle:], earlier_ref[:middle]], 0)
    near_ref[...] = jnp.where(first, later, earlier).astype(jnp.bfloat16)
    far_ref[...] = jnp.where(first, earlier, later).astype(jnp.bfloat16)


def attend_kernel(piece_ref, query_ref, key_ref, out_ref, wide_ref, turned_ref):
    wide_ref[...] = piece_ref[...].astype(jnp.float32)
    channels = wide_ref.shape[0]
    tiles, _ = turned(channels)
    for place in range(8):
        parity, half = place // 2, place % 2
        columns = slice(half * 128, (half + 1) * 128)
        for run in range(0, channels, 8):
            start = parity * channels + tiles[run]
            turned_ref[start : start + 8, columns] = wide_ref[run : run + 8, place, :]
    wide = turned_ref[...].T
    tokens = wide.astype(jnp.bfloat16)
    queries = jnp.dot(tokens, query_ref[...], preferred_element_type=jnp.float32).astype(jnp.bfloat16)
    keys = jnp.dot(tokens, key_ref[...], preferred_element_type=jnp.float32).astype(jnp.bfloat16)
    scores = lax.dot_general(queries, keys, (((1,), (1,)), ((), ())), preferred_element_type=jnp.float32)
    scores = scores * (tokens.shape[1] ** -0.5)
    raised = jnp.exp(scores - jnp.max(scores, axis=1, keepdims=True))
    weights = (raised / jnp.sum(raised, axis=1, keepdims=True)).astype(jnp.bfloat16)
    mixed = jnp.dot(weights, tokens, preferred_element_type=jnp.float32)
    out_ref[...] = (wide + mixed).astype(jnp.bfloat16)


def local(latent, conv_weight, conv_bias, query_weight, key_weight):
    tiles = lax.axis_size("tile")
    channels = conv_weight.shape[0]
    core = lax.axis_index("core").astype(jnp.int32)
    copies = jnp.broadcast_to(latent, (tiles,) + latent.shape[1:])
    order, _ = turned(tiles)
    gathered = lax.all_to_all(copies, "tile", split_axis=0, concat_axis=0, tiled=True, axis_index_groups=[order])
    rows = jnp.transpose(conv_weight, (1, 2, 3, 0, 4)).reshape(-1, conv_weight.shape[-1])
    head = lax.axis_index("tile") % HEADS
    query_rows = lax.dynamic_index_in_dim(query_weight, head, 0, keepdims=False)
    key_rows = lax.dynamic_index_in_dim(key_weight, head, 0, keepdims=False)

    edge = jax.ShapeDtypeStruct((channels, 8, 128), jnp.bfloat16)
    own, near, far = pl.pallas_call(
        conv_kernel,
        out_shape=(jax.ShapeDtypeStruct((2, channels, 8, 128), jnp.float32), edge, edge),
        in_specs=[pl.BlockSpec(memory_space=pltpu.SMEM)] + [pl.BlockSpec(memory_space=pltpu.VMEM)] * 3,
        out_specs=[pl.BlockSpec(memory_space=pltpu.VMEM)] * 3,
        scratch_shapes=[pltpu.VMEM((channels, 8, 128), jnp.float32)] * 2,
        compiler_params=pltpu.CompilerParams(vmem_limit_bytes=VMEM_LIMIT),
        name="conv",
    )(core.reshape(1), rows, gathered, conv_bias.reshape(channels, 1))

    groups = lax.axis_size("pair") * lax.axis_size("core")
    route = [(t, t + 1) for t in range(1, groups - 1, 2)] + [(t + 1, t) for t in range(1, groups - 1, 2)]
    from_far = lax.ppermute(far, TM, route)
    both = lax.all_gather(near, "core", axis=0)
    from_near = jnp.where(core == 0, both[1], both[0])
    to_first = jnp.where(core == 0, from_far, from_near).astype(jnp.float32)
    to_second = jnp.where(core == 0, from_near, from_far).astype(jnp.float32)
    frames = (own + jnp.stack([to_first, to_second])).astype(jnp.bfloat16)
    received = lax.all_to_all(
        frames.reshape(2 * channels, 8, 128), "tile", split_axis=0, concat_axis=0, tiled=True, axis_index_groups=[order]
    )
    vmem = pl.BlockSpec(memory_space=pltpu.VMEM)
    attended = pl.pallas_call(
        attend_kernel,
        out_shape=jax.ShapeDtypeStruct((CELLS, 4 * tiles), jnp.bfloat16),
        in_specs=[vmem] * 3,
        out_specs=vmem,
        scratch_shapes=[pltpu.VMEM((tiles, 8, 128), jnp.float32), pltpu.VMEM((4 * tiles, CELLS), jnp.float32)],
        compiler_params=pltpu.CompilerParams(vmem_limit_bytes=VMEM_LIMIT),
        name="attend",
    )(received, query_rows, key_rows)
    return attended[None]


def solution(mesh):
    split = Mesh(mesh.devices.reshape(-1, 2, mesh.devices.shape[1]), ("pair", "core", "tile"))
    in_specs = (P(TM, "tile", None), P("tile", None, None, None, None), P("tile"), P(), P())
    out_specs = P(TM + ("tile",), None, None)
    return jax.shard_map(local, mesh=split, in_specs=in_specs, out_specs=out_specs, check_vma=False)
```

```python
import jax
import jax.numpy as jnp
from jax import lax
from jax.experimental import pallas as pl
from jax.experimental.pallas import tpu as pltpu
from jax.sharding import Mesh, PartitionSpec as P

HEADS = 16
SIDE = 16
CELLS = SIDE * SIDE
TM = ("pair", "core")
TILE = ("xl", "z")
VMEM_LIMIT = 32 * 1024 * 1024


def turned(order):
    half = order // 2
    tiles = [start + (z + half // 2) % half for start in (0, half) for z in range(half)]
    return tiles, [tiles.index(tile) for tile in range(order)]


def in_turn(blocks, places):
    return jnp.concatenate([blocks[place] for place in places], 0)


def spread(tap_slabs, channels):
    lane = lax.broadcasted_iota(jnp.int32, (channels, CELLS), 1)
    row, col = lane // SIDE, lane % SIDE
    for pa in (0, 1):
        for pb in (0, 1):
            total = None
            for ky, dy in ((1, 0), (3, -1)) if pa == 0 else ((2, 0), (0, 1)):
                for kx, dx in ((1, 0), (3, -1)) if pb == 0 else ((2, 0), (0, 1)):
                    slab = tap_slabs(ky, kx)
                    step = dy * SIDE + dx
                    if step:
                        slab = pltpu.roll(slab, (-step) % CELLS, 1)
                        inside = (row + dy >= 0) & (row + dy < SIDE) & (col + dx >= 0) & (col + dx < SIDE)
                        slab = jnp.where(inside, slab, 0.0)
                    total = slab if total is None else total + slab
            yield pa, pb, total


def conv_kernel(core_ref, weight_ref, latent_ref, bias_ref, own_ref, near_ref, far_ref, later_ref, earlier_ref):
    channels = bias_ref.shape[0]
    rows = 16 * channels
    _, places = turned(latent_ref.shape[0])
    latent = in_turn(latent_ref, places)
    for kt in (3, 0, 1, 2):
        products = jnp.dot(
            weight_ref[kt * rows : (kt + 1) * rows, :], latent, preferred_element_type=jnp.float32
        )

        def tap(ky, kx):
            start = (ky * 4 + kx) * channels
            return products[start : start + channels, :]

        for pa, pb, total in spread(tap, channels):
            if kt in (1, 2):
                total = total + bias_ref[...]
            for half in (0, 1):
                piece = total[:, half * 128 : (half + 1) * 128]
                place = (pa * 2 + pb) * 2 + half
                if kt == 3:
                    later_ref[:, place, :] = piece
                elif kt == 0:
                    earlier_ref[:, place, :] = piece
                else:
                    middle = channels // 2
                    own_ref[kt - 1, :middle, place, :] = piece[middle:]
                    own_ref[kt - 1, middle:, place, :] = piece[:middle]
    first = core_ref[0] == 0
    middle = channels // 2
    later = jnp.concatenate([later_ref[middle:], later_ref[:middle]], 0)
    earlier = jnp.concatenate([earlier_ref[middle:], earlier_ref[:middle]], 0)
    near_ref[...] = jnp.where(first, later, earlier).astype(jnp.bfloat16)
    far_ref[...] = jnp.where(first, earlier, later).astype(jnp.bfloat16)


def attend_kernel(piece_ref, query_ref, key_ref, out_ref, wide_ref, turned_ref):
    wide_ref[...] = piece_ref[...].astype(jnp.float32)
    channels = wide_ref.shape[0]
    tiles, _ = turned(channels)
    for place in range(8):
        parity, half = place // 2, place % 2
        columns = slice(half * 128, (half + 1) * 128)
        for run in range(0, channels, 8):
            start = parity * channels + tiles[run]
            turned_ref[start : start + 8, columns] = wide_ref[run : run + 8, place, :]
    wide = turned_ref[...].T
    tokens = wide.astype(jnp.bfloat16)
    queries = jnp.dot(tokens, query_ref[...], preferred_element_type=jnp.float32).astype(jnp.bfloat16)
    keys = jnp.dot(tokens, key_ref[...], preferred_element_type=jnp.float32).astype(jnp.bfloat16)
    scores = lax.dot_general(queries, keys, (((1,), (1,)), ((), ())), preferred_element_type=jnp.float32)
    scores = scores * (tokens.shape[1] ** -0.5)
    raised = jnp.exp(scores - jnp.max(scores, axis=1, keepdims=True))
    weights = (raised / jnp.sum(raised, axis=1, keepdims=True)).astype(jnp.bfloat16)
    mixed = jnp.dot(weights, tokens, preferred_element_type=jnp.float32)
    out_ref[...] = (wide + mixed).astype(jnp.bfloat16)


def local(latent, conv_weight, conv_bias, query_weight, key_weight):
    tiles = lax.axis_size(TILE)
    channels = conv_weight.shape[0]
    core = lax.axis_index("core").astype(jnp.int32)
    depth = lax.axis_size("z")
    order, _ = turned(tiles)
    copies = jnp.broadcast_to(latent, (depth,) + latent.shape[1:])
    column = lax.all_to_all(
        copies, "z", split_axis=0, concat_axis=0, tiled=True, axis_index_groups=[order[:depth]]
    )
    gathered = lax.all_gather(column, "xl", axis=0, tiled=True)
    rows = jnp.transpose(conv_weight, (1, 2, 3, 0, 4)).reshape(-1, conv_weight.shape[-1])
    head = lax.axis_index(TILE) % HEADS
    query_rows = lax.dynamic_index_in_dim(query_weight, head, 0, keepdims=False)
    key_rows = lax.dynamic_index_in_dim(key_weight, head, 0, keepdims=False)

    edge = jax.ShapeDtypeStruct((channels, 8, 128), jnp.bfloat16)
    own, near, far = pl.pallas_call(
        conv_kernel,
        out_shape=(jax.ShapeDtypeStruct((2, channels, 8, 128), jnp.float32), edge, edge),
        in_specs=[pl.BlockSpec(memory_space=pltpu.SMEM)] + [pl.BlockSpec(memory_space=pltpu.VMEM)] * 3,
        out_specs=[pl.BlockSpec(memory_space=pltpu.VMEM)] * 3,
        scratch_shapes=[pltpu.VMEM((channels, 8, 128), jnp.float32)] * 2,
        compiler_params=pltpu.CompilerParams(vmem_limit_bytes=VMEM_LIMIT),
        name="conv",
    )(core.reshape(1), rows, gathered, conv_bias.reshape(channels, 1))

    groups = lax.axis_size("pair") * lax.axis_size("core")
    route = [(t, t + 1) for t in range(1, groups - 1, 2)] + [(t + 1, t) for t in range(1, groups - 1, 2)]
    from_far = lax.ppermute(far, TM, route)
    both = lax.all_gather(near, "core", axis=0)
    from_near = jnp.where(core == 0, both[1], both[0])
    to_first = jnp.where(core == 0, from_far, from_near).astype(jnp.float32)
    to_second = jnp.where(core == 0, from_near, from_far).astype(jnp.float32)
    frames = (own + jnp.stack([to_first, to_second])).astype(jnp.bfloat16)
    received = lax.all_to_all(
        frames.reshape(2 * channels, 8, 128), TILE, split_axis=0, concat_axis=0, tiled=True, axis_index_groups=[order]
    )
    vmem = pl.BlockSpec(memory_space=pltpu.VMEM)
    attended = pl.pallas_call(
        attend_kernel,
        out_shape=jax.ShapeDtypeStruct((CELLS, 4 * tiles), jnp.bfloat16),
        in_specs=[vmem] * 3,
        out_specs=vmem,
        scratch_shapes=[pltpu.VMEM((tiles, 8, 128), jnp.float32), pltpu.VMEM((4 * tiles, CELLS), jnp.float32)],
        compiler_params=pltpu.CompilerParams(vmem_limit_bytes=VMEM_LIMIT),
        name="attend",
    )(received, query_rows, key_rows)
    return attended[None]


def solution(mesh):
    split = Mesh(mesh.devices.reshape(-1, 2, 2, mesh.devices.shape[1] // 2), TM + TILE)
    in_specs = (P(TM, TILE, None), P(TILE, None, None, None, None), P(TILE), P(), P())
    out_specs = P(TM + TILE, None, None)
    return jax.shard_map(local, mesh=split, in_specs=in_specs, out_specs=out_specs, check_vma=False)
```

```python
import jax
import jax.numpy as jnp
from jax import lax
from jax.experimental import pallas as pl
from jax.experimental.pallas import tpu as pltpu
from jax.sharding import Mesh, PartitionSpec as P

HEADS = 16
SIDE = 16
CELLS = SIDE * SIDE
TM = ("pair", "core")
TILE = ("xl", "z")
VMEM_LIMIT = 32 * 1024 * 1024


FIRST_GATHER, FIRST_FRAMES = 8, 8


def turned(order, first):
    half = order // 2
    tiles = [start + (z + first) % half for start in (0, half) for z in range(half)]
    return tiles, [tiles.index(tile) for tile in range(order)]


def in_turn(blocks, places):
    return jnp.concatenate([blocks[place] for place in places], 0)


def spread(tap_slabs, channels):
    lane = lax.broadcasted_iota(jnp.int32, (channels, CELLS), 1)
    row, col = lane // SIDE, lane % SIDE
    for pa in (0, 1):
        for pb in (0, 1):
            total = None
            for ky, dy in ((1, 0), (3, -1)) if pa == 0 else ((2, 0), (0, 1)):
                for kx, dx in ((1, 0), (3, -1)) if pb == 0 else ((2, 0), (0, 1)):
                    slab = tap_slabs(ky, kx)
                    step = dy * SIDE + dx
                    if step:
                        slab = pltpu.roll(slab, (-step) % CELLS, 1)
                        inside = (row + dy >= 0) & (row + dy < SIDE) & (col + dx >= 0) & (col + dx < SIDE)
                        slab = jnp.where(inside, slab, 0.0)
                    total = slab if total is None else total + slab
            yield pa, pb, total


def conv_kernel(core_ref, weight_ref, latent_ref, bias_ref, own_ref, near_ref, far_ref, later_ref, earlier_ref):
    channels = bias_ref.shape[0]
    rows = 16 * channels
    _, places = turned(latent_ref.shape[0], FIRST_GATHER)
    latent = in_turn(latent_ref, places)
    for kt in (3, 0, 1, 2):
        products = jnp.dot(
            weight_ref[kt * rows : (kt + 1) * rows, :], latent, preferred_element_type=jnp.float32
        )

        def tap(ky, kx):
            start = (ky * 4 + kx) * channels
            return products[start : start + channels, :]

        for pa, pb, total in spread(tap, channels):
            if kt in (1, 2):
                total = total + bias_ref[...]
            for half in (0, 1):
                piece = total[:, half * 128 : (half + 1) * 128]
                place = (pa * 2 + pb) * 2 + half
                if kt == 3:
                    later_ref[:, place, :] = piece
                elif kt == 0:
                    earlier_ref[:, place, :] = piece
                else:
                    own_ref[kt - 1, : channels - FIRST_FRAMES, place, :] = piece[FIRST_FRAMES:]
                    own_ref[kt - 1, channels - FIRST_FRAMES :, place, :] = piece[:FIRST_FRAMES]
    first = core_ref[0] == 0
    later = jnp.concatenate([later_ref[FIRST_FRAMES:], later_ref[:FIRST_FRAMES]], 0)
    earlier = jnp.concatenate([earlier_ref[FIRST_FRAMES:], earlier_ref[:FIRST_FRAMES]], 0)
    near_ref[...] = jnp.where(first, later, earlier).astype(jnp.bfloat16)
    far_ref[...] = jnp.where(first, earlier, later).astype(jnp.bfloat16)


def attend_kernel(piece_ref, query_ref, key_ref, out_ref, wide_ref, turned_ref):
    wide_ref[...] = piece_ref[...].astype(jnp.float32)
    channels = wide_ref.shape[0]
    column = channels // 2
    runs = [
        (start + skip, start + (skip + FIRST_FRAMES) % column, size)
        for start in (0, column)
        for skip, size in ((0, column - FIRST_FRAMES), (column - FIRST_FRAMES, FIRST_FRAMES))
        if size
    ]
    for place in range(8):
        parity, half = place // 2, place % 2
        columns = slice(half * 128, (half + 1) * 128)
        for source, target, size in runs:
            start = parity * channels + target
            turned_ref[start : start + size, columns] = wide_ref[source : source + size, place, :]
    wide = turned_ref[...].T
    tokens = wide.astype(jnp.bfloat16)
    queries = jnp.dot(tokens, query_ref[...], preferred_element_type=jnp.float32).astype(jnp.bfloat16)
    keys = jnp.dot(tokens, key_ref[...], preferred_element_type=jnp.float32).astype(jnp.bfloat16)
    scores = lax.dot_general(queries, keys, (((1,), (1,)), ((), ())), preferred_element_type=jnp.float32)
    scores = scores * (tokens.shape[1] ** -0.5)
    raised = jnp.exp(scores - jnp.max(scores, axis=1, keepdims=True))
    weights = (raised / jnp.sum(raised, axis=1, keepdims=True)).astype(jnp.bfloat16)
    mixed = jnp.dot(weights, tokens, preferred_element_type=jnp.float32)
    out_ref[...] = (wide + mixed).astype(jnp.bfloat16)


def local(latent, conv_weight, conv_bias, query_weight, key_weight):
    tiles = lax.axis_size(TILE)
    channels = conv_weight.shape[0]
    core = lax.axis_index("core").astype(jnp.int32)
    depth = lax.axis_size("z")
    gather_order, _ = turned(tiles, FIRST_GATHER)
    frames_order, _ = turned(tiles, FIRST_FRAMES)
    copies = jnp.broadcast_to(latent, (depth,) + latent.shape[1:])
    column = lax.all_to_all(
        copies, "z", split_axis=0, concat_axis=0, tiled=True, axis_index_groups=[gather_order[:depth]]
    )
    gathered = lax.all_gather(column, "xl", axis=0, tiled=True)
    rows = jnp.transpose(conv_weight, (1, 2, 3, 0, 4)).reshape(-1, conv_weight.shape[-1])
    head = lax.axis_index(TILE) % HEADS
    query_rows = lax.dynamic_index_in_dim(query_weight, head, 0, keepdims=False)
    key_rows = lax.dynamic_index_in_dim(key_weight, head, 0, keepdims=False)

    rows, query_rows, key_rows = lax.optimization_barrier((rows, query_rows, key_rows))

    edge = jax.ShapeDtypeStruct((channels, 8, 128), jnp.bfloat16)
    own, near, far = pl.pallas_call(
        conv_kernel,
        out_shape=(jax.ShapeDtypeStruct((2, channels, 8, 128), jnp.float32), edge, edge),
        in_specs=[pl.BlockSpec(memory_space=pltpu.SMEM)] + [pl.BlockSpec(memory_space=pltpu.VMEM)] * 3,
        out_specs=[pl.BlockSpec(memory_space=pltpu.VMEM)] * 3,
        scratch_shapes=[pltpu.VMEM((channels, 8, 128), jnp.float32)] * 2,
        compiler_params=pltpu.CompilerParams(vmem_limit_bytes=VMEM_LIMIT),
        name="conv",
    )(core.reshape(1), rows, gathered, conv_bias.reshape(channels, 1))

    groups = lax.axis_size("pair") * lax.axis_size("core")
    route = [(t, t + 1) for t in range(1, groups - 1, 2)] + [(t + 1, t) for t in range(1, groups - 1, 2)]
    from_far = lax.ppermute(far, TM, route)
    both = lax.all_gather(near, "core", axis=0)
    from_near = jnp.where(core == 0, both[1], both[0])
    to_first = jnp.where(core == 0, from_far, from_near).astype(jnp.float32)
    to_second = jnp.where(core == 0, from_near, from_far).astype(jnp.float32)
    frames = (own + jnp.stack([to_first, to_second])).astype(jnp.bfloat16)
    received = lax.all_to_all(
        frames.reshape(2 * channels, 8, 128), TILE, split_axis=0, concat_axis=0, tiled=True, axis_index_groups=[frames_order]
    )
    vmem = pl.BlockSpec(memory_space=pltpu.VMEM)
    attended = pl.pallas_call(
        attend_kernel,
        out_shape=jax.ShapeDtypeStruct((CELLS, 4 * tiles), jnp.bfloat16),
        in_specs=[vmem] * 3,
        out_specs=vmem,
        scratch_shapes=[pltpu.VMEM((tiles, 8, 128), jnp.float32), pltpu.VMEM((4 * tiles, CELLS), jnp.float32)],
        compiler_params=pltpu.CompilerParams(vmem_limit_bytes=VMEM_LIMIT),
        name="attend",
    )(received, query_rows, key_rows)
    return attended[None]


def solution(mesh):
    split = Mesh(mesh.devices.reshape(-1, 2, 2, mesh.devices.shape[1] // 2), TM + TILE)
    in_specs = (P(TM, TILE, None), P(TILE, None, None, None, None), P(TILE), P(), P())
    out_specs = P(TM + TILE, None, None)
    return jax.shard_map(local, mesh=split, in_specs=in_specs, out_specs=out_specs, check_vma=False)
```

```python
import jax
import jax.numpy as jnp
from jax import lax
from jax.experimental import pallas as pl
from jax.experimental.pallas import tpu as pltpu
from jax.sharding import Mesh, PartitionSpec as P

HEADS = 16
SIDE = 16
CELLS = SIDE * SIDE
TM = ("pair", "core")
TILE = ("xl", "z")
VMEM_LIMIT = 32 * 1024 * 1024


FIRST_GATHER, FIRST_FRAMES = 10, 8


def turned(order, first):
    half = order // 2
    tiles = [start + (z + first) % half for start in (0, half) for z in range(half)]
    return tiles, [tiles.index(tile) for tile in range(order)]


def in_turn(blocks, places):
    return jnp.concatenate([blocks[place] for place in places], 0)


def spread(tap_slabs, channels):
    lane = lax.broadcasted_iota(jnp.int32, (channels, CELLS), 1)
    row, col = lane // SIDE, lane % SIDE
    for pa in (0, 1):
        for pb in (0, 1):
            total = None
            for ky, dy in ((1, 0), (3, -1)) if pa == 0 else ((2, 0), (0, 1)):
                for kx, dx in ((1, 0), (3, -1)) if pb == 0 else ((2, 0), (0, 1)):
                    slab = tap_slabs(ky, kx)
                    step = dy * SIDE + dx
                    if step:
                        slab = pltpu.roll(slab, (-step) % CELLS, 1)
                        inside = (row + dy >= 0) & (row + dy < SIDE) & (col + dx >= 0) & (col + dx < SIDE)
                        slab = jnp.where(inside, slab, 0.0)
                    total = slab if total is None else total + slab
            yield pa, pb, total


def conv_kernel(weight_ref, latent_ref, bias_ref, out_ref, wide_ref):
    channels = bias_ref.shape[0]
    rows = 16 * channels
    after = channels - FIRST_FRAMES
    _, places = turned(latent_ref.shape[0], FIRST_GATHER)
    latent = in_turn(latent_ref, places)
    for kt, frame, kind in ((1, 0, 0), (2, 1, 0), (3, 0, 1), (0, 1, 1)):
        products = jnp.dot(
            weight_ref[kt * rows : (kt + 1) * rows, :], latent, preferred_element_type=jnp.float32
        )

        def tap(ky, kx):
            start = (ky * 4 + kx) * channels
            return products[start : start + channels, :]

        for pa, pb, total in spread(tap, channels):
            if kind == 0:
                total = total + bias_ref[...]
            for half in (0, 1):
                piece = total[:, half * 128 : (half + 1) * 128]
                place = kind * 8 + (pa * 2 + pb) * 2 + half
                wide_ref[frame, :after, place, :] = piece[FIRST_FRAMES:]
                wide_ref[frame, after:, place, :] = piece[:FIRST_FRAMES]
    out_ref[...] = wide_ref[...].astype(jnp.bfloat16)


def attend_kernel(piece_ref, edge_ref, query_ref, key_ref, out_ref, wide_ref, turned_ref):
    wide_ref[...] = piece_ref[:, :8, :].astype(jnp.float32) + edge_ref[...].astype(jnp.float32)
    channels = wide_ref.shape[0]
    column = channels // 2
    runs = [
        (start + skip, start + (skip + FIRST_FRAMES) % column, size)
        for start in (0, column)
        for skip, size in ((0, column - FIRST_FRAMES), (column - FIRST_FRAMES, FIRST_FRAMES))
        if size
    ]
    for place in range(8):
        parity, half = place // 2, place % 2
        columns = slice(half * 128, (half + 1) * 128)
        for source, target, size in runs:
            start = parity * channels + target
            turned_ref[start : start + size, columns] = wide_ref[source : source + size, place, :]
    tokens = turned_ref[...].T.astype(jnp.bfloat16)
    wide = tokens.astype(jnp.float32)
    queries = jnp.dot(tokens, query_ref[...], preferred_element_type=jnp.float32).astype(jnp.bfloat16)
    keys = jnp.dot(tokens, key_ref[...], preferred_element_type=jnp.float32).astype(jnp.bfloat16)
    scores = lax.dot_general(queries, keys, (((1,), (1,)), ((), ())), preferred_element_type=jnp.float32)
    scores = scores * (tokens.shape[1] ** -0.5)
    raised = jnp.exp(scores - jnp.max(scores, axis=1, keepdims=True))
    weights = (raised / jnp.sum(raised, axis=1, keepdims=True)).astype(jnp.bfloat16)
    mixed = jnp.dot(weights, tokens, preferred_element_type=jnp.float32)
    out_ref[...] = (wide + mixed).astype(jnp.bfloat16)


def local(latent, conv_weight, conv_bias, query_weight, key_weight):
    tiles = lax.axis_size(TILE)
    channels = conv_weight.shape[0]
    core = lax.axis_index("core").astype(jnp.int32)
    depth = lax.axis_size("z")
    gather_order, _ = turned(tiles, FIRST_GATHER)
    frames_order, _ = turned(tiles, FIRST_FRAMES)
    copies = jnp.broadcast_to(latent, (depth,) + latent.shape[1:])
    column = lax.all_to_all(
        copies, "z", split_axis=0, concat_axis=0, tiled=True, axis_index_groups=[gather_order[:depth]]
    )
    gathered = lax.all_gather(column, "xl", axis=0, tiled=True)
    rows = jnp.transpose(conv_weight, (1, 2, 3, 0, 4)).reshape(-1, conv_weight.shape[-1])
    head = lax.axis_index(TILE) % HEADS
    query_rows = lax.dynamic_index_in_dim(query_weight, head, 0, keepdims=False)
    key_rows = lax.dynamic_index_in_dim(key_weight, head, 0, keepdims=False)

    rows, query_rows, key_rows = lax.optimization_barrier((rows, query_rows, key_rows))

    vmem = pl.BlockSpec(memory_space=pltpu.VMEM)
    params = pltpu.CompilerParams(vmem_limit_bytes=VMEM_LIMIT)
    frames = pl.pallas_call(
        conv_kernel,
        out_shape=jax.ShapeDtypeStruct((2, channels, 16, 128), jnp.bfloat16),
        in_specs=[vmem] * 3,
        out_specs=vmem,
        scratch_shapes=[pltpu.VMEM((2, channels, 16, 128), jnp.float32)],
        compiler_params=params,
        name="conv",
    )(rows, gathered, conv_bias.reshape(channels, 1))
    received = lax.all_to_all(
        frames.reshape(2 * channels, 16, 128),
        TILE,
        split_axis=0,
        concat_axis=0,
        tiled=True,
        axis_index_groups=[frames_order],
    )

    edge = received[:, 8:, :]
    groups = lax.axis_size(TM)
    column = lax.axis_index("xl")
    forward = [(t * tiles + z, (t + 2) * tiles + z) for t in range(1, groups - 2, 2) for z in range(depth)]
    backward = [(t * tiles + z, (t - 1) * tiles + z) for t in range(2, groups, 2) for z in range(depth, tiles)]
    relayed = lax.ppermute(edge, TM + TILE, forward)
    direct = lax.ppermute(edge, TM + TILE, backward)
    shown = jnp.where((core == 1) & (column == 0), relayed, edge)
    both = lax.all_gather(shown, "core", axis=0)
    other = jnp.where(core == 0, both[1], both[0])
    edge = jnp.where((core == 1) & (column == 1), direct, other)
    attended = pl.pallas_call(
        attend_kernel,
        out_shape=jax.ShapeDtypeStruct((CELLS, 4 * tiles), jnp.bfloat16),
        in_specs=[vmem] * 4,
        out_specs=vmem,
        scratch_shapes=[pltpu.VMEM((tiles, 8, 128), jnp.float32), pltpu.VMEM((4 * tiles, CELLS), jnp.float32)],
        compiler_params=pltpu.CompilerParams(vmem_limit_bytes=VMEM_LIMIT),
        name="attend",
    )(received, edge, query_rows, key_rows)
    return attended[None]


def solution(mesh):
    split = Mesh(mesh.devices.reshape(-1, 2, 2, mesh.devices.shape[1] // 2), TM + TILE)
    in_specs = (P(TM, TILE, None), P(TILE, None, None, None, None), P(TILE), P(), P())
    out_specs = P(TM + TILE, None, None)
    return jax.shard_map(local, mesh=split, in_specs=in_specs, out_specs=out_specs, check_vma=False)
```

```python
import jax
import jax.numpy as jnp
from jax import lax
from jax.experimental import pallas as pl
from jax.experimental.pallas import tpu as pltpu
from jax.sharding import Mesh, PartitionSpec as P

HEADS = 16
SIDE = 16
CELLS = SIDE * SIDE
TM = ("pair", "core")
TILE = ("xl", "z")
VMEM_LIMIT = 32 * 1024 * 1024


FIRST_GATHER, FIRST_FRAMES = 11, 8


def turned(order, first):
    half = order // 2
    tiles = [start + (z + first) % half for start in (0, half) for z in range(half)]
    return tiles, [tiles.index(tile) for tile in range(order)]


def in_turn(blocks, places):
    return jnp.concatenate([blocks[place] for place in places], 0)


def spread(tap_slabs, channels):
    lane = lax.broadcasted_iota(jnp.int32, (channels, CELLS), 1)
    row, col = lane // SIDE, lane % SIDE
    for pa in (0, 1):
        for pb in (0, 1):
            total = None
            for ky, dy in ((1, 0), (3, -1)) if pa == 0 else ((2, 0), (0, 1)):
                for kx, dx in ((1, 0), (3, -1)) if pb == 0 else ((2, 0), (0, 1)):
                    slab = tap_slabs(ky, kx)
                    step = dy * SIDE + dx
                    if step:
                        slab = pltpu.roll(slab, (-step) % CELLS, 1)
                        inside = (row + dy >= 0) & (row + dy < SIDE) & (col + dx >= 0) & (col + dx < SIDE)
                        slab = jnp.where(inside, slab, 0.0)
                    total = slab if total is None else total + slab
            yield pa, pb, total


def conv_kernel(weight_ref, latent_ref, bias_ref, out_ref, wide_ref):
    channels = bias_ref.shape[0]
    rows = 16 * channels
    after = channels - FIRST_FRAMES
    _, places = turned(latent_ref.shape[0], FIRST_GATHER)
    latent = in_turn(latent_ref, places)
    for kt, frame, kind in ((1, 0, 0), (2, 1, 0), (3, 0, 1), (0, 1, 1)):
        products = jnp.dot(
            weight_ref[kt * rows : (kt + 1) * rows, :], latent, preferred_element_type=jnp.float32
        )

        def tap(ky, kx):
            start = (ky * 4 + kx) * channels
            return products[start : start + channels, :]

        for pa, pb, total in spread(tap, channels):
            if kind == 0:
                total = total + bias_ref[...]
            for half in (0, 1):
                piece = total[:, half * 128 : (half + 1) * 128]
                place = kind * 8 + (pa * 2 + pb) * 2 + half
                wide_ref[frame, :after, place, :] = piece[FIRST_FRAMES:]
                wide_ref[frame, after:, place, :] = piece[:FIRST_FRAMES]
    out_ref[...] = wide_ref[...].astype(jnp.bfloat16)


def attend_kernel(piece_ref, edge_ref, query_ref, key_ref, out_ref, wide_ref, turned_ref):
    wide_ref[...] = piece_ref[:, :8, :].astype(jnp.float32) + edge_ref[...].astype(jnp.float32)
    channels = wide_ref.shape[0]
    column = channels // 2
    runs = [
        (start + skip, start + (skip + FIRST_FRAMES) % column, size)
        for start in (0, column)
        for skip, size in ((0, column - FIRST_FRAMES), (column - FIRST_FRAMES, FIRST_FRAMES))
        if size
    ]
    for place in range(8):
        parity, half = place // 2, place % 2
        columns = slice(half * 128, (half + 1) * 128)
        for source, target, size in runs:
            start = parity * channels + target
            turned_ref[start : start + size, columns] = wide_ref[source : source + size, place, :]
    across = turned_ref[...].astype(jnp.bfloat16)
    wide = across.astype(jnp.float32).T
    tokens = wide.astype(jnp.bfloat16)
    contract_first = (((0,), (0,)), ((), ()))
    queries = lax.dot_general(query_ref[...], across, contract_first, preferred_element_type=jnp.float32)
    keys = jnp.dot(tokens, key_ref[...], preferred_element_type=jnp.float32)
    scores = jnp.dot(keys.astype(jnp.bfloat16), queries.astype(jnp.bfloat16), preferred_element_type=jnp.float32)
    scores = scores * (tokens.shape[1] ** -0.5)
    raised = jnp.exp(scores - jnp.max(scores, axis=0, keepdims=True))
    weights = (raised / jnp.sum(raised, axis=0, keepdims=True)).astype(jnp.bfloat16)
    mixed = jnp.dot(across, weights, preferred_element_type=jnp.float32)
    out_ref[...] = (wide + mixed.T).astype(jnp.bfloat16)


def local(latent, conv_weight, conv_bias, query_weight, key_weight):
    tiles = lax.axis_size(TILE)
    channels = conv_weight.shape[0]
    core = lax.axis_index("core").astype(jnp.int32)
    depth = lax.axis_size("z")
    gather_order, _ = turned(tiles, FIRST_GATHER)
    frames_order, _ = turned(tiles, FIRST_FRAMES)
    copies = jnp.broadcast_to(latent, (depth,) + latent.shape[1:])
    column = lax.all_to_all(
        copies, "z", split_axis=0, concat_axis=0, tiled=True, axis_index_groups=[gather_order[:depth]]
    )
    gathered = lax.all_gather(column, "xl", axis=0, tiled=True)
    rows = jnp.transpose(conv_weight, (1, 2, 3, 0, 4)).reshape(-1, conv_weight.shape[-1])
    head = lax.axis_index(TILE) % HEADS
    query_rows = lax.dynamic_index_in_dim(query_weight, head, 0, keepdims=False)
    key_rows = lax.dynamic_index_in_dim(key_weight, head, 0, keepdims=False)

    rows, query_rows, key_rows = lax.optimization_barrier((rows, query_rows, key_rows))

    vmem = pl.BlockSpec(memory_space=pltpu.VMEM)
    params = pltpu.CompilerParams(vmem_limit_bytes=VMEM_LIMIT)
    frames = pl.pallas_call(
        conv_kernel,
        out_shape=jax.ShapeDtypeStruct((2, channels, 16, 128), jnp.bfloat16),
        in_specs=[vmem] * 3,
        out_specs=vmem,
        scratch_shapes=[pltpu.VMEM((2, channels, 16, 128), jnp.float32)],
        compiler_params=params,
        name="conv",
    )(rows, gathered, conv_bias.reshape(channels, 1))
    received = lax.all_to_all(
        frames.reshape(2 * channels, 16, 128),
        TILE,
        split_axis=0,
        concat_axis=0,
        tiled=True,
        axis_index_groups=[frames_order],
    )

    edge = received[:, 8:, :]
    groups = lax.axis_size(TM)
    column = lax.axis_index("xl")
    forward = [(t * tiles + z, (t + 2) * tiles + z) for t in range(1, groups - 2, 2) for z in range(depth)]
    backward = [(t * tiles + z, (t - 1) * tiles + z) for t in range(2, groups, 2) for z in range(depth, tiles)]
    relayed = lax.ppermute(edge, TM + TILE, forward)
    direct = lax.ppermute(edge, TM + TILE, backward)
    shown = jnp.where((core == 1) & (column == 0), relayed, edge)
    both = lax.all_gather(shown, "core", axis=0)
    other = jnp.where(core == 0, both[1], both[0])
    edge = jnp.where((core == 1) & (column == 1), direct, other)
    attended = pl.pallas_call(
        attend_kernel,
        out_shape=jax.ShapeDtypeStruct((CELLS, 4 * tiles), jnp.bfloat16),
        in_specs=[vmem] * 4,
        out_specs=vmem,
        scratch_shapes=[pltpu.VMEM((tiles, 8, 128), jnp.float32), pltpu.VMEM((4 * tiles, CELLS), jnp.float32)],
        compiler_params=pltpu.CompilerParams(vmem_limit_bytes=VMEM_LIMIT),
        name="attend",
    )(received, edge, query_rows, key_rows)
    return attended[None]


def solution(mesh):
    split = Mesh(mesh.devices.reshape(-1, 2, 2, mesh.devices.shape[1] // 2), TM + TILE)
    in_specs = (P(TM, TILE, None), P(TILE, None, None, None, None), P(TILE), P(), P())
    out_specs = P(TM + TILE, None, None)
    return jax.shard_map(local, mesh=split, in_specs=in_specs, out_specs=out_specs, check_vma=False)
```

```python
import jax
import jax.numpy as jnp
from jax import lax
from jax.experimental import pallas as pl
from jax.experimental.pallas import tpu as pltpu
from jax.sharding import Mesh, PartitionSpec as P

HEADS = 16
SIDE = 16
CELLS = SIDE * SIDE
TM = ("pair", "core")
TILE = ("xl", "z")
VMEM_LIMIT = 32 * 1024 * 1024


FIRST_GATHER, FIRST_FRAMES = 11, 8


def turned(order, first):
    half = order // 2
    tiles = [start + (z + first) % half for start in (0, half) for z in range(half)]
    return tiles, [tiles.index(tile) for tile in range(order)]


def in_turn(blocks, places):
    return jnp.concatenate([blocks[place] for place in places], 0)


def spread(tap_slabs, channels):
    lane = lax.broadcasted_iota(jnp.int32, (channels, CELLS), 1)
    row, col = lane // SIDE, lane % SIDE
    for pa in (0, 1):
        for pb in (0, 1):
            total = None
            for ky, dy in ((1, 0), (3, -1)) if pa == 0 else ((2, 0), (0, 1)):
                for kx, dx in ((1, 0), (3, -1)) if pb == 0 else ((2, 0), (0, 1)):
                    slab = tap_slabs(ky, kx)
                    step = dy * SIDE + dx
                    if step:
                        slab = pltpu.roll(slab, (-step) % CELLS, 1)
                        inside = (row + dy >= 0) & (row + dy < SIDE) & (col + dx >= 0) & (col + dx < SIDE)
                        slab = jnp.where(inside, slab, 0.0)
                    total = slab if total is None else total + slab
            yield pa, pb, total


def conv_kernel(weight_ref, latent_ref, bias_ref, own_ref, next_ref, last_ref, later_ref, earlier_ref):
    channels = bias_ref.shape[0]
    rows = 16 * channels
    _, places = turned(latent_ref.shape[0], FIRST_GATHER)
    latent = in_turn(latent_ref, places)
    for kt in (3, 0, 1, 2):
        products = jnp.dot(
            weight_ref[kt * rows : (kt + 1) * rows, :], latent, preferred_element_type=jnp.float32
        )

        def tap(ky, kx):
            start = (ky * 4 + kx) * channels
            return products[start : start + channels, :]

        for pa, pb, total in spread(tap, channels):
            if kt in (1, 2):
                total = total + bias_ref[...]
            for half in (0, 1):
                piece = total[:, half * 128 : (half + 1) * 128]
                place = (pa * 2 + pb) * 2 + half
                if kt == 3:
                    later_ref[:, place, :] = piece
                elif kt == 0:
                    earlier_ref[:, place, :] = piece
                else:
                    own_ref[kt - 1, : channels - FIRST_FRAMES, place, :] = piece[FIRST_FRAMES:]
                    own_ref[kt - 1, channels - FIRST_FRAMES :, place, :] = piece[:FIRST_FRAMES]
    later = jnp.concatenate([later_ref[FIRST_FRAMES:], later_ref[:FIRST_FRAMES]], 0)
    earlier = jnp.concatenate([earlier_ref[FIRST_FRAMES:], earlier_ref[:FIRST_FRAMES]], 0)
    next_ref[...] = later
    last_ref[...] = earlier.astype(jnp.bfloat16)


def leave_kernel(own_ref, next_ref, last_ref):
    pass


def attend_kernel(piece_ref, query_ref, key_ref, out_ref, wide_ref, turned_ref):
    wide_ref[...] = piece_ref[...].astype(jnp.float32)
    channels = wide_ref.shape[0]
    column = channels // 2
    runs = [
        (start + skip, start + (skip + FIRST_FRAMES) % column, size)
        for start in (0, column)
        for skip, size in ((0, column - FIRST_FRAMES), (column - FIRST_FRAMES, FIRST_FRAMES))
        if size
    ]
    for place in range(8):
        parity, half = place // 2, place % 2
        columns = slice(half * 128, (half + 1) * 128)
        for source, target, size in runs:
            start = parity * channels + target
            turned_ref[start : start + size, columns] = wide_ref[source : source + size, place, :]
    across = turned_ref[...]
    wide = across.T
    tokens, across = wide.astype(jnp.bfloat16), across.astype(jnp.bfloat16)
    contract_first = (((0,), (0,)), ((), ()))
    queries = lax.dot_general(query_ref[...], across, contract_first, preferred_element_type=jnp.float32)
    keys = jnp.dot(tokens, key_ref[...], preferred_element_type=jnp.float32)
    scores = jnp.dot(keys.astype(jnp.bfloat16), queries.astype(jnp.bfloat16), preferred_element_type=jnp.float32)
    scores = scores * (tokens.shape[1] ** -0.5)
    raised = jnp.exp(scores - jnp.max(scores, axis=0, keepdims=True))
    weights = (raised / jnp.sum(raised, axis=0, keepdims=True)).astype(jnp.bfloat16)
    mixed = jnp.dot(across, weights, preferred_element_type=jnp.float32)
    out_ref[...] = (wide + mixed.T).astype(jnp.bfloat16)


def local(latent, conv_weight, conv_bias, query_weight, key_weight):
    tiles = lax.axis_size(TILE)
    channels = conv_weight.shape[0]
    core = lax.axis_index("core").astype(jnp.int32)
    depth = lax.axis_size("z")
    gather_order, _ = turned(tiles, FIRST_GATHER)
    frames_order, _ = turned(tiles, FIRST_FRAMES)
    copies = jnp.broadcast_to(latent, (depth,) + latent.shape[1:])
    column = lax.all_to_all(
        copies, "z", split_axis=0, concat_axis=0, tiled=True, axis_index_groups=[gather_order[:depth]]
    )
    rows = jnp.transpose(conv_weight, (1, 2, 3, 0, 4)).reshape(-1, conv_weight.shape[-1])
    head = lax.axis_index(TILE) % HEADS
    query_rows = lax.dynamic_index_in_dim(query_weight, head, 0, keepdims=False)
    key_rows = lax.dynamic_index_in_dim(key_weight, head, 0, keepdims=False)

    rows, query_rows, key_rows = lax.optimization_barrier((rows, query_rows, key_rows))

    vmem = pl.BlockSpec(memory_space=pltpu.VMEM)
    edge = jax.ShapeDtypeStruct((channels, 8, 128), jnp.bfloat16)
    shapes = (
        jax.ShapeDtypeStruct((2, channels, 8, 128), jnp.float32),
        jax.ShapeDtypeStruct(edge.shape, jnp.float32),
        edge,
    )
    biases = conv_bias.reshape(channels, 1)

    def work(column, rows, biases):
        gathered = lax.all_gather(column, "xl", axis=0, tiled=True)
        return tuple(
            pl.pallas_call(
                conv_kernel,
                out_shape=shapes,
                in_specs=[vmem] * 3,
                out_specs=[vmem] * 3,
                scratch_shapes=[pltpu.VMEM((channels, 8, 128), jnp.float32)] * 2,
                compiler_params=pltpu.CompilerParams(vmem_limit_bytes=VMEM_LIMIT),
                name="conv",
            )(rows, gathered, biases)
        )

    def leave(column, rows, biases):
        return tuple(
            pl.pallas_call(
                leave_kernel, out_shape=shapes, out_specs=[pl.BlockSpec(memory_space=pl.ANY)] * 3, name="leave"
            )()
        )

    ones = lax.cond(core == 1, work, leave, column, rows, biases)
    groups = lax.axis_size("pair") * lax.axis_size("core")
    from_last = lax.ppermute(ones[1], TM, [(t, t + 1) for t in range(1, groups - 1, 2)])
    column, ones = lax.optimization_barrier((column, ones))
    zeros = lax.cond(core == 0, work, leave, column, rows, biases)
    own = jnp.where(core == 0, zeros[0], ones[0])
    to_next, to_last = zeros[1], jnp.where(core == 0, zeros[2], ones[2])
    from_next = lax.ppermute(zeros[2], TM, [(t, t - 1) for t in range(2, groups, 2)])
    both = lax.all_gather(jnp.where(core == 0, to_next.astype(jnp.bfloat16), to_last), "core", axis=0)
    to_first = jnp.where(core == 0, from_last, both[0].astype(jnp.float32))
    to_second = jnp.where(core == 0, both[1], from_next).astype(jnp.float32)
    frames = (own + jnp.stack([to_first, to_second])).astype(jnp.bfloat16)
    received = lax.all_to_all(
        frames.reshape(2 * channels, 8, 128), TILE, split_axis=0, concat_axis=0, tiled=True, axis_index_groups=[frames_order]
    )
    vmem = pl.BlockSpec(memory_space=pltpu.VMEM)
    attended = pl.pallas_call(
        attend_kernel,
        out_shape=jax.ShapeDtypeStruct((CELLS, 4 * tiles), jnp.bfloat16),
        in_specs=[vmem] * 3,
        out_specs=vmem,
        scratch_shapes=[pltpu.VMEM((tiles, 8, 128), jnp.float32), pltpu.VMEM((4 * tiles, CELLS), jnp.float32)],
        compiler_params=pltpu.CompilerParams(vmem_limit_bytes=VMEM_LIMIT),
        name="attend",
    )(received, query_rows, key_rows)
    return attended[None]


def solution(mesh):
    split = Mesh(mesh.devices.reshape(-1, 2, 2, mesh.devices.shape[1] // 2), TM + TILE)
    in_specs = (P(TM, TILE, None), P(TILE, None, None, None, None), P(TILE), P(), P())
    out_specs = P(TM + TILE, None, None)
    return jax.shard_map(local, mesh=split, in_specs=in_specs, out_specs=out_specs, check_vma=False)
```

```python
import jax
import jax.numpy as jnp
from jax import lax
from jax.experimental import pallas as pl
from jax.experimental.pallas import tpu as pltpu
from jax.sharding import Mesh, PartitionSpec as P

HEADS = 16
SIDE = 16
CELLS = SIDE * SIDE
TM = ("pair", "core")
TILE = ("xl", "z")
VMEM_LIMIT = 32 * 1024 * 1024


FIRST_GATHER, FIRST_FRAMES = 11, 8


def turned(order, first):
    half = order // 2
    tiles = [start + (z + first) % half for start in (0, half) for z in range(half)]
    return tiles, [tiles.index(tile) for tile in range(order)]


def in_turn(blocks, places):
    return jnp.concatenate([blocks[place] for place in places], 0)


def spread(tap_slabs, channels):
    lane = lax.broadcasted_iota(jnp.int32, (channels, CELLS), 1)
    row, col = lane // SIDE, lane % SIDE
    for pa in (0, 1):
        for pb in (0, 1):
            total = None
            for ky, dy in ((1, 0), (3, -1)) if pa == 0 else ((2, 0), (0, 1)):
                for kx, dx in ((1, 0), (3, -1)) if pb == 0 else ((2, 0), (0, 1)):
                    slab = tap_slabs(ky, kx)
                    step = dy * SIDE + dx
                    if step:
                        slab = pltpu.roll(slab, (-step) % CELLS, 1)
                        inside = (row + dy >= 0) & (row + dy < SIDE) & (col + dx >= 0) & (col + dx < SIDE)
                        slab = jnp.where(inside, slab, 0.0)
                    total = slab if total is None else total + slab
            yield pa, pb, total


def conv_kernel(weight_ref, latent_ref, bias_ref, own_ref, next_ref, last_ref, later_ref, earlier_ref):
    channels = bias_ref.shape[0]
    rows = 16 * channels
    _, places = turned(latent_ref.shape[0], FIRST_GATHER)
    latent = in_turn(latent_ref, places)
    for kt in (3, 0, 1, 2):
        products = jnp.dot(
            weight_ref[kt * rows : (kt + 1) * rows, :], latent, preferred_element_type=jnp.float32
        )

        def tap(ky, kx):
            start = (ky * 4 + kx) * channels
            return products[start : start + channels, :]

        for pa, pb, total in spread(tap, channels):
            if kt in (1, 2):
                total = total + bias_ref[...]
            for half in (0, 1):
                piece = total[:, half * 128 : (half + 1) * 128]
                place = (pa * 2 + pb) * 2 + half
                if kt == 3:
                    later_ref[:, place, :] = piece
                elif kt == 0:
                    earlier_ref[:, place, :] = piece
                else:
                    own_ref[kt - 1, : channels - FIRST_FRAMES, place, :] = piece[FIRST_FRAMES:]
                    own_ref[kt - 1, channels - FIRST_FRAMES :, place, :] = piece[:FIRST_FRAMES]
    later = jnp.concatenate([later_ref[FIRST_FRAMES:], later_ref[:FIRST_FRAMES]], 0)
    earlier = jnp.concatenate([earlier_ref[FIRST_FRAMES:], earlier_ref[:FIRST_FRAMES]], 0)
    next_ref[...] = later.astype(jnp.bfloat16)
    last_ref[...] = earlier.astype(jnp.bfloat16)


def leave_kernel(own_ref, next_ref, last_ref):
    pass


def attend_kernel(piece_ref, query_ref, key_ref, out_ref, wide_ref, turned_ref):
    wide_ref[...] = piece_ref[...].astype(jnp.float32)
    channels = wide_ref.shape[0]
    column = channels // 2
    runs = [
        (start + skip, start + (skip + FIRST_FRAMES) % column, size)
        for start in (0, column)
        for skip, size in ((0, column - FIRST_FRAMES), (column - FIRST_FRAMES, FIRST_FRAMES))
        if size
    ]
    for place in range(8):
        parity, half = place // 2, place % 2
        columns = slice(half * 128, (half + 1) * 128)
        for source, target, size in runs:
            start = parity * channels + target
            turned_ref[start : start + size, columns] = wide_ref[source : source + size, place, :]
    across = turned_ref[...]
    wide = across.T
    tokens, across = wide.astype(jnp.bfloat16), across.astype(jnp.bfloat16)
    contract_first = (((0,), (0,)), ((), ()))
    queries = lax.dot_general(query_ref[...], across, contract_first, preferred_element_type=jnp.float32)
    keys = jnp.dot(tokens, key_ref[...], preferred_element_type=jnp.float32)
    scores = jnp.dot(keys.astype(jnp.bfloat16), queries.astype(jnp.bfloat16), preferred_element_type=jnp.float32)
    scores = scores * (tokens.shape[1] ** -0.5)
    raised = jnp.exp(scores - jnp.max(scores, axis=0, keepdims=True))
    weights = (raised / jnp.sum(raised, axis=0, keepdims=True)).astype(jnp.bfloat16)
    mixed = jnp.dot(across, weights, preferred_element_type=jnp.float32)
    out_ref[...] = (wide + mixed.T).astype(jnp.bfloat16)


def local(latent, conv_weight, conv_bias, query_weight, key_weight):
    tiles = lax.axis_size(TILE)
    channels = conv_weight.shape[0]
    core = lax.axis_index("core").astype(jnp.int32)
    depth = lax.axis_size("z")
    gather_order, _ = turned(tiles, FIRST_GATHER)
    frames_order, _ = turned(tiles, FIRST_FRAMES)
    copies = jnp.broadcast_to(latent, (depth,) + latent.shape[1:])
    column = lax.all_to_all(
        copies, "z", split_axis=0, concat_axis=0, tiled=True, axis_index_groups=[gather_order[:depth]]
    )
    rows = jnp.transpose(conv_weight, (1, 2, 3, 0, 4)).reshape(-1, conv_weight.shape[-1])
    head = lax.axis_index(TILE) % HEADS
    query_rows = lax.dynamic_index_in_dim(query_weight, head, 0, keepdims=False)
    key_rows = lax.dynamic_index_in_dim(key_weight, head, 0, keepdims=False)

    rows, query_rows, key_rows = lax.optimization_barrier((rows, query_rows, key_rows))

    vmem = pl.BlockSpec(memory_space=pltpu.VMEM)
    edge = jax.ShapeDtypeStruct((channels, 8, 128), jnp.bfloat16)
    shapes = (jax.ShapeDtypeStruct((2, channels, 8, 128), jnp.float32), edge, edge)
    biases = conv_bias.reshape(channels, 1)

    def work(column, rows, biases):
        gathered = lax.all_gather(column, "xl", axis=0, tiled=True)
        return tuple(
            pl.pallas_call(
                conv_kernel,
                out_shape=shapes,
                in_specs=[vmem] * 3,
                out_specs=[vmem] * 3,
                scratch_shapes=[pltpu.VMEM((channels, 8, 128), jnp.float32)] * 2,
                compiler_params=pltpu.CompilerParams(vmem_limit_bytes=VMEM_LIMIT),
                name="conv",
            )(rows, gathered, biases)
        )

    def leave(column, rows, biases):
        return tuple(
            pl.pallas_call(
                leave_kernel, out_shape=shapes, out_specs=[pl.BlockSpec(memory_space=pl.ANY)] * 3, name="leave"
            )()
        )

    ones = lax.cond(core == 1, work, leave, column, rows, biases)
    groups = lax.axis_size("pair") * lax.axis_size("core")
    from_last = lax.ppermute(ones[1], TM, [(t, t + 1) for t in range(1, groups - 1, 2)])
    column, ones = lax.optimization_barrier((column, ones))
    zeros = lax.cond(core == 0, work, leave, column, rows, biases)
    own = jnp.where(core == 0, zeros[0], ones[0])
    to_next, to_last = zeros[1], jnp.where(core == 0, zeros[2], ones[2])
    from_next = lax.ppermute(zeros[2], TM, [(t, t - 1) for t in range(2, groups, 2)])
    both = lax.all_gather(jnp.where(core == 0, to_next, to_last), "core", axis=0)
    to_first = jnp.where(core == 0, from_last, both[0]).astype(jnp.float32)
    to_second = jnp.where(core == 0, both[1], from_next).astype(jnp.float32)
    frames = (own + jnp.stack([to_first, to_second])).astype(jnp.bfloat16)
    received = lax.all_to_all(
        frames.reshape(2 * channels, 8, 128), TILE, split_axis=0, concat_axis=0, tiled=True, axis_index_groups=[frames_order]
    )
    vmem = pl.BlockSpec(memory_space=pltpu.VMEM)
    attended = pl.pallas_call(
        attend_kernel,
        out_shape=jax.ShapeDtypeStruct((CELLS, 4 * tiles), jnp.bfloat16),
        in_specs=[vmem] * 3,
        out_specs=vmem,
        scratch_shapes=[pltpu.VMEM((tiles, 8, 128), jnp.float32), pltpu.VMEM((4 * tiles, CELLS), jnp.float32)],
        compiler_params=pltpu.CompilerParams(vmem_limit_bytes=VMEM_LIMIT),
        name="attend",
    )(received, query_rows, key_rows)
    return attended[None]


def solution(mesh):
    split = Mesh(mesh.devices.reshape(-1, 2, 2, mesh.devices.shape[1] // 2), TM + TILE)
    in_specs = (P(TM, TILE, None), P(TILE, None, None, None, None), P(TILE), P(), P())
    out_specs = P(TM + TILE, None, None)
    return jax.shard_map(local, mesh=split, in_specs=in_specs, out_specs=out_specs, check_vma=False)
```

```python
import jax
import jax.numpy as jnp
from jax import lax
from jax.experimental import pallas as pl
from jax.experimental.pallas import tpu as pltpu
from jax.sharding import Mesh, PartitionSpec as P

HEADS = 16
SIDE = 16
CELLS = SIDE * SIDE
TM = ("pair", "core")
TILE = ("xl", "z")
VMEM_LIMIT = 32 * 1024 * 1024


FIRST_GATHER, FIRST_FRAMES = 10, 10


def turned(order, first):
    half = order // 2
    tiles = [start + (z + first) % half for start in (0, half) for z in range(half)]
    return tiles, [tiles.index(tile) for tile in range(order)]


def in_turn(blocks, places):
    return jnp.concatenate([blocks[place] for place in places], 0)


def spread(tap_slabs, channels):
    lane = lax.broadcasted_iota(jnp.int32, (channels, CELLS), 1)
    row, col = lane // SIDE, lane % SIDE
    for pa in (0, 1):
        for pb in (0, 1):
            total = None
            for ky, dy in ((1, 0), (3, -1)) if pa == 0 else ((2, 0), (0, 1)):
                for kx, dx in ((1, 0), (3, -1)) if pb == 0 else ((2, 0), (0, 1)):
                    slab = tap_slabs(ky, kx)
                    step = dy * SIDE + dx
                    if step:
                        slab = pltpu.roll(slab, (-step) % CELLS, 1)
                        inside = (row + dy >= 0) & (row + dy < SIDE) & (col + dx >= 0) & (col + dx < SIDE)
                        slab = jnp.where(inside, slab, 0.0)
                    total = slab if total is None else total + slab
            yield pa, pb, total


def conv_kernel(weight_ref, latent_ref, bias_ref, own_ref, next_ref, last_ref, later_ref, earlier_ref):
    channels = bias_ref.shape[0]
    rows = 16 * channels
    _, places = turned(latent_ref.shape[0], FIRST_GATHER)
    latent = in_turn(latent_ref, places)
    for kt in (3, 0, 1, 2):
        products = jnp.dot(
            weight_ref[kt * rows : (kt + 1) * rows, :], latent, preferred_element_type=jnp.float32
        )

        def tap(ky, kx):
            start = (ky * 4 + kx) * channels
            return products[start : start + channels, :]

        for pa, pb, total in spread(tap, channels):
            if kt in (1, 2):
                total = total + bias_ref[...]
            for half in (0, 1):
                piece = total[:, half * 128 : (half + 1) * 128]
                place = (pa * 2 + pb) * 2 + half
                if kt == 3:
                    later_ref[:, place, :] = piece
                elif kt == 0:
                    earlier_ref[:, place, :] = piece
                else:
                    own_ref[kt - 1, : channels - FIRST_FRAMES, place, :] = piece[FIRST_FRAMES:]
                    own_ref[kt - 1, channels - FIRST_FRAMES :, place, :] = piece[:FIRST_FRAMES]
    later = jnp.concatenate([later_ref[FIRST_FRAMES:], later_ref[:FIRST_FRAMES]], 0)
    earlier = jnp.concatenate([earlier_ref[FIRST_FRAMES:], earlier_ref[:FIRST_FRAMES]], 0)
    next_ref[...] = later.astype(jnp.bfloat16)
    last_ref[...] = earlier.astype(jnp.bfloat16)


def leave_kernel(own_ref, next_ref, last_ref):
    pass


def attend_kernel(piece_ref, query_ref, key_ref, out_ref, wide_ref, turned_ref):
    wide_ref[...] = piece_ref[...].astype(jnp.float32)
    channels = wide_ref.shape[0]
    column = channels // 2
    runs = [
        (start + skip, start + (skip + FIRST_FRAMES) % column, size)
        for start in (0, column)
        for skip, size in ((0, column - FIRST_FRAMES), (column - FIRST_FRAMES, FIRST_FRAMES))
        if size
    ]
    for place in range(8):
        parity, half = place // 2, place % 2
        columns = slice(half * 128, (half + 1) * 128)
        for source, target, size in runs:
            start = parity * channels + target
            turned_ref[start : start + size, columns] = wide_ref[source : source + size, place, :]
    across = turned_ref[...]
    wide = across.T
    tokens, across = wide.astype(jnp.bfloat16), across.astype(jnp.bfloat16)
    contract_first = (((0,), (0,)), ((), ()))
    queries = lax.dot_general(query_ref[...], across, contract_first, preferred_element_type=jnp.float32)
    keys = jnp.dot(tokens, key_ref[...], preferred_element_type=jnp.float32)
    scores = jnp.dot(keys.astype(jnp.bfloat16), queries.astype(jnp.bfloat16), preferred_element_type=jnp.float32)
    scores = scores * (tokens.shape[1] ** -0.5)
    raised = jnp.exp(scores - jnp.max(scores, axis=0, keepdims=True))
    weights = (raised / jnp.sum(raised, axis=0, keepdims=True)).astype(jnp.bfloat16)
    mixed = jnp.dot(across, weights, preferred_element_type=jnp.float32)
    out_ref[...] = (wide + mixed.T).astype(jnp.bfloat16)


def local(latent, conv_weight, conv_bias, query_weight, key_weight):
    tiles = lax.axis_size(TILE)
    channels = conv_weight.shape[0]
    core = lax.axis_index("core").astype(jnp.int32)
    depth = lax.axis_size("z")
    gather_order, _ = turned(tiles, FIRST_GATHER)
    frames_order, _ = turned(tiles, FIRST_FRAMES)
    copies = jnp.broadcast_to(latent, (depth,) + latent.shape[1:])
    column = lax.all_to_all(
        copies, "z", split_axis=0, concat_axis=0, tiled=True, axis_index_groups=[gather_order[:depth]]
    )
    rows = jnp.transpose(conv_weight, (1, 2, 3, 0, 4)).reshape(-1, conv_weight.shape[-1])
    head = lax.axis_index(TILE) % HEADS
    query_rows = lax.dynamic_index_in_dim(query_weight, head, 0, keepdims=False)
    key_rows = lax.dynamic_index_in_dim(key_weight, head, 0, keepdims=False)

    rows, query_rows, key_rows = lax.optimization_barrier((rows, query_rows, key_rows))

    vmem = pl.BlockSpec(memory_space=pltpu.VMEM)
    edge = jax.ShapeDtypeStruct((channels, 8, 128), jnp.bfloat16)
    shapes = (jax.ShapeDtypeStruct((2, channels, 8, 128), jnp.float32), edge, edge)
    biases = conv_bias.reshape(channels, 1)

    def work(column, rows, biases):
        gathered = lax.all_gather(column, "xl", axis=0, tiled=True)
        return tuple(
            pl.pallas_call(
                conv_kernel,
                out_shape=shapes,
                in_specs=[vmem] * 3,
                out_specs=[vmem] * 3,
                scratch_shapes=[pltpu.VMEM((channels, 8, 128), jnp.float32)] * 2,
                compiler_params=pltpu.CompilerParams(vmem_limit_bytes=VMEM_LIMIT),
                name="conv",
            )(rows, gathered, biases)
        )

    def leave(column, rows, biases):
        return tuple(
            pl.pallas_call(
                leave_kernel, out_shape=shapes, out_specs=[pl.BlockSpec(memory_space=pl.ANY)] * 3, name="leave"
            )()
        )

    ones = lax.cond(core == 1, work, leave, column, rows, biases)
    groups = lax.axis_size("pair") * lax.axis_size("core")
    from_last = lax.ppermute(ones[1], TM, [(t, t + 1) for t in range(1, groups - 1, 2)])
    column, ones = lax.optimization_barrier((column, ones))
    zeros = lax.cond(core == 0, work, leave, column, rows, biases)
    own = jnp.where(core == 0, zeros[0], ones[0])
    to_next, to_last = zeros[1], jnp.where(core == 0, zeros[2], ones[2])
    from_next = lax.ppermute(zeros[2], TM, [(t, t - 1) for t in range(2, groups, 2)])
    both = lax.all_gather(jnp.where(core == 0, to_next, to_last), "core", axis=0)
    to_first = jnp.where(core == 0, from_last, both[0]).astype(jnp.float32)
    to_second = jnp.where(core == 0, both[1], from_next).astype(jnp.float32)
    frames = (own + jnp.stack([to_first, to_second])).astype(jnp.bfloat16)
    received = lax.all_to_all(
        frames.reshape(2 * channels, 8, 128), TILE, split_axis=0, concat_axis=0, tiled=True, axis_index_groups=[frames_order]
    )
    vmem = pl.BlockSpec(memory_space=pltpu.VMEM)
    attended = pl.pallas_call(
        attend_kernel,
        out_shape=jax.ShapeDtypeStruct((CELLS, 4 * tiles), jnp.bfloat16),
        in_specs=[vmem] * 3,
        out_specs=vmem,
        scratch_shapes=[pltpu.VMEM((tiles, 8, 128), jnp.float32), pltpu.VMEM((4 * tiles, CELLS), jnp.float32)],
        compiler_params=pltpu.CompilerParams(vmem_limit_bytes=VMEM_LIMIT),
        name="attend",
    )(received, query_rows, key_rows)
    return attended[None]


def solution(mesh):
    split = Mesh(mesh.devices.reshape(-1, 2, 2, mesh.devices.shape[1] // 2), TM + TILE)
    in_specs = (P(TM, TILE, None), P(TILE, None, None, None, None), P(TILE), P(), P())
    out_specs = P(TM + TILE, None, None)
    return jax.shard_map(local, mesh=split, in_specs=in_specs, out_specs=out_specs, check_vma=False)
```

```python
import jax
import jax.numpy as jnp
from jax import lax
from jax.experimental import pallas as pl
from jax.experimental.pallas import tpu as pltpu
from jax.sharding import Mesh, PartitionSpec as P

HEADS = 16
SIDE = 16
CELLS = SIDE * SIDE
TM = ("pair", "core")
TILE = ("xl", "z")
VMEM_LIMIT = 32 * 1024 * 1024


FIRST_GATHER, FIRST_FRAMES = 10, 10


def turned(order, first):
    half = order // 2
    tiles = [start + (z + first) % half for start in (0, half) for z in range(half)]
    return tiles, [tiles.index(tile) for tile in range(order)]


def in_turn(blocks, places):
    return jnp.concatenate([blocks[place] for place in places], 0)


def spread(tap_slabs, channels):
    lane = lax.broadcasted_iota(jnp.int32, (channels, CELLS), 1)
    row, col = lane // SIDE, lane % SIDE
    for pa in (0, 1):
        for pb in (0, 1):
            total = None
            for ky, dy in ((1, 0), (3, -1)) if pa == 0 else ((2, 0), (0, 1)):
                for kx, dx in ((1, 0), (3, -1)) if pb == 0 else ((2, 0), (0, 1)):
                    slab = tap_slabs(ky, kx)
                    step = dy * SIDE + dx
                    if step:
                        slab = pltpu.roll(slab, (-step) % CELLS, 1)
                        inside = (row + dy >= 0) & (row + dy < SIDE) & (col + dx >= 0) & (col + dx < SIDE)
                        slab = jnp.where(inside, slab, 0.0)
                    total = slab if total is None else total + slab
            yield pa, pb, total


def conv_kernel(weight_ref, latent_ref, bias_ref, own_ref, next_ref, last_ref, later_ref, earlier_ref):
    channels = bias_ref.shape[0]
    rows = 16 * channels
    _, places = turned(latent_ref.shape[0], FIRST_GATHER)
    latent = in_turn(latent_ref, places)
    for kt in (3, 0, 1, 2):
        products = jnp.dot(
            weight_ref[kt * rows : (kt + 1) * rows, :], latent, preferred_element_type=jnp.float32
        )

        def tap(ky, kx):
            start = (ky * 4 + kx) * channels
            return products[start : start + channels, :]

        for pa, pb, total in spread(tap, channels):
            if kt in (1, 2):
                total = total + bias_ref[...]
            for half in (0, 1):
                piece = total[:, half * 128 : (half + 1) * 128]
                place = (pa * 2 + pb) * 2 + half
                if kt == 3:
                    later_ref[:, place, :] = piece
                elif kt == 0:
                    earlier_ref[:, place, :] = piece
                else:
                    own_ref[kt - 1, : channels - FIRST_FRAMES, place, :] = piece[FIRST_FRAMES:]
                    own_ref[kt - 1, channels - FIRST_FRAMES :, place, :] = piece[:FIRST_FRAMES]
    later = jnp.concatenate([later_ref[FIRST_FRAMES:], later_ref[:FIRST_FRAMES]], 0)
    earlier = jnp.concatenate([earlier_ref[FIRST_FRAMES:], earlier_ref[:FIRST_FRAMES]], 0)
    next_ref[...] = later.astype(jnp.bfloat16)
    last_ref[...] = earlier.astype(jnp.bfloat16)


def leave_kernel(own_ref, next_ref, last_ref):
    pass


def attend_kernel(piece_ref, query_ref, key_ref, out_ref, wide_ref, turned_ref):
    wide_ref[...] = piece_ref[...].astype(jnp.float32)
    channels = wide_ref.shape[0]
    column = channels // 2
    runs = [
        (start + skip, start + (skip + FIRST_FRAMES) % column, size)
        for start in (0, column)
        for skip, size in ((0, column - FIRST_FRAMES), (column - FIRST_FRAMES, FIRST_FRAMES))
        if size
    ]
    for place in range(8):
        parity, half = place // 2, place % 2
        columns = slice(half * 128, (half + 1) * 128)
        for source, target, size in runs:
            start = parity * channels + target
            turned_ref[start : start + size, columns] = wide_ref[source : source + size, place, :]
    across = turned_ref[...]
    wide, across = across, across.astype(jnp.bfloat16)
    tokens = across.T
    contract_first = (((0,), (0,)), ((), ()))
    queries = lax.dot_general(query_ref[...], across, contract_first, preferred_element_type=jnp.float32)
    keys = jnp.dot(tokens, key_ref[...], preferred_element_type=jnp.float32)
    scores = jnp.dot(keys.astype(jnp.bfloat16), queries.astype(jnp.bfloat16), preferred_element_type=jnp.float32)
    scores = scores * (tokens.shape[1] ** -0.5)
    raised = jnp.exp(scores - jnp.max(scores, axis=0, keepdims=True))
    weights = (raised / jnp.sum(raised, axis=0, keepdims=True)).astype(jnp.bfloat16)
    mixed = jnp.dot(across, weights, preferred_element_type=jnp.float32)
    out_ref[...] = (wide + mixed).T.astype(jnp.bfloat16)


def local(latent, conv_weight, conv_bias, query_weight, key_weight):
    tiles = lax.axis_size(TILE)
    channels = conv_weight.shape[0]
    core = lax.axis_index("core").astype(jnp.int32)
    depth = lax.axis_size("z")
    gather_order, _ = turned(tiles, FIRST_GATHER)
    frames_order, _ = turned(tiles, FIRST_FRAMES)
    copies = jnp.broadcast_to(latent, (depth,) + latent.shape[1:])
    column = lax.all_to_all(
        copies, "z", split_axis=0, concat_axis=0, tiled=True, axis_index_groups=[gather_order[:depth]]
    )
    rows = jnp.transpose(conv_weight, (1, 2, 3, 0, 4)).reshape(-1, conv_weight.shape[-1])
    head = lax.axis_index(TILE) % HEADS
    query_rows = lax.dynamic_index_in_dim(query_weight, head, 0, keepdims=False)
    key_rows = lax.dynamic_index_in_dim(key_weight, head, 0, keepdims=False)

    rows, query_rows, key_rows = lax.optimization_barrier((rows, query_rows, key_rows))

    vmem = pl.BlockSpec(memory_space=pltpu.VMEM)
    edge = jax.ShapeDtypeStruct((channels, 8, 128), jnp.bfloat16)
    shapes = (jax.ShapeDtypeStruct((2, channels, 8, 128), jnp.float32), edge, edge)
    biases = conv_bias.reshape(channels, 1)

    def work(column, rows, biases):
        gathered = lax.all_gather(column, "xl", axis=0, tiled=True)
        return tuple(
            pl.pallas_call(
                conv_kernel,
                out_shape=shapes,
                in_specs=[vmem] * 3,
                out_specs=[vmem] * 3,
                scratch_shapes=[pltpu.VMEM((channels, 8, 128), jnp.float32)] * 2,
                compiler_params=pltpu.CompilerParams(vmem_limit_bytes=VMEM_LIMIT),
                name="conv",
            )(rows, gathered, biases)
        )

    def leave(column, rows, biases):
        return tuple(
            pl.pallas_call(
                leave_kernel, out_shape=shapes, out_specs=[pl.BlockSpec(memory_space=pl.ANY)] * 3, name="leave"
            )()
        )

    ones = lax.cond(core == 1, work, leave, column, rows, biases)
    groups = lax.axis_size("pair") * lax.axis_size("core")
    from_last = lax.ppermute(ones[1], TM, [(t, t + 1) for t in range(1, groups - 1, 2)])
    column, ones = lax.optimization_barrier((column, ones))
    zeros = lax.cond(core == 0, work, leave, column, rows, biases)
    own = jnp.where(core == 0, zeros[0], ones[0])
    to_next, to_last = zeros[1], jnp.where(core == 0, zeros[2], ones[2])
    from_next = lax.ppermute(zeros[2], TM, [(t, t - 1) for t in range(2, groups, 2)])
    both = lax.all_gather(jnp.where(core == 0, to_next, to_last), "core", axis=0)
    to_first = jnp.where(core == 0, from_last, both[0]).astype(jnp.float32)
    to_second = jnp.where(core == 0, both[1], from_next).astype(jnp.float32)
    frames = (own + jnp.stack([to_first, to_second])).astype(jnp.bfloat16)
    received = lax.all_to_all(
        frames.reshape(2 * channels, 8, 128), TILE, split_axis=0, concat_axis=0, tiled=True, axis_index_groups=[frames_order]
    )
    vmem = pl.BlockSpec(memory_space=pltpu.VMEM)
    attended = pl.pallas_call(
        attend_kernel,
        out_shape=jax.ShapeDtypeStruct((CELLS, 4 * tiles), jnp.bfloat16),
        in_specs=[vmem] * 3,
        out_specs=vmem,
        scratch_shapes=[pltpu.VMEM((tiles, 8, 128), jnp.float32), pltpu.VMEM((4 * tiles, CELLS), jnp.float32)],
        compiler_params=pltpu.CompilerParams(vmem_limit_bytes=VMEM_LIMIT),
        name="attend",
    )(received, query_rows, key_rows)
    return attended[None]


def solution(mesh):
    split = Mesh(mesh.devices.reshape(-1, 2, 2, mesh.devices.shape[1] // 2), TM + TILE)
    in_specs = (P(TM, TILE, None), P(TILE, None, None, None, None), P(TILE), P(), P())
    out_specs = P(TM + TILE, None, None)
    return jax.shard_map(local, mesh=split, in_specs=in_specs, out_specs=out_specs, check_vma=False)
```
